256 devices in a mesh: blk: 16 (over z, y_lo), grp: 16 (over x, y_hi, core).
Axes of the slice: x: 4, y: 4 (y_hi: 2, y_lo: 2; y = y_hi * 2 + y_lo), z: 8, core: 2. Of those that a mesh axis runs over, the one named last changes fastest.
Arguments:
- state: float32 [2, 128, 32768], P(None, None, ('blk', 'grp')), may hold values from -3 to 3
- prev_slope: float32 [2, 128, 32768], P(None, None, ('blk', 'grp')), may hold values from -4 to 4
- positions: float32 [2, 32768], P(None, ('blk', 'grp')), may hold values from -1 to 1
- pump: float32 [32768], P(('blk', 'grp')), may hold values from -0.5 to 1.5
- detuning: float32 [32768], P(('blk', 'grp')), may hold values from -4 to 4
- kappa: float32 [6, 32768], P(None, ('blk', 'grp')), may hold values from 0.2 to 1
- neighbours: int32 [6, 32768], P(None, ('blk', 'grp')), may hold values from 0 to 255
- send_list: int32 [2, 16384], P(None, ('blk', 'grp')), may hold values from 0 to 127
Outputs:
- slope: float32 [2, 128, 32768], P(None, None, ('blk', 'grp'))
The draws below stay inside these ranges and needn't reach their ends.
Inputs may be any that keep to these rules, and one draw needn't show every extreme that they name: `neighbours`: places below 128 are the block's own emitters, the next 64 those listed by the previous block, the last 64 those listed by the next block. `send_list`: places in the listing block.
All inputs are finite; a program needn't handle non-finite values.
Results may differ from the reference program's by a relative error of at most 0.0012.
Values may be sent and summed in bfloat16 or wider, within the bound.
A program may use at most 64 MiB of HBM per device.

```python
import math
import jax
import jax.numpy as jnp
from jax import lax

ROWS = 128
MEMBERS = 128
NEIGH = 6
HALO = 64
EMITTERS = 32768
DEVICES = 256


def with_ends(result, key, least, high):
    spot = [jax.random.randint(jax.random.fold_in(key, axis), (), 0, length) for axis, length in enumerate(result.shape)]
    widest = result.shape.index(max(result.shape))
    neighbour = spot[:widest] + [(spot[widest] + 1) % result.shape[widest]] + spot[widest + 1:]
    return result.at[tuple(spot)].set(least).at[tuple(neighbour)].set(high)


def level_of(key, extent, shards, low, largest):
    def one(dim, blocks):
        heights = jax.random.uniform(jax.random.fold_in(jax.random.fold_in(key, 6), dim), (blocks,), jnp.float32, low / len(shards), largest / len(shards))
        return jnp.repeat(jnp.exp(heights), extent[dim] // blocks).reshape((-1,) + (1,) * (len(extent) - dim - 1))

    loudness = one(*shards[0])
    for cut in shards[1:]:
        loudness = loudness * one(*cut)
    return loudness


def scatter_about(rng, shape, width, limit, pieces=(), kind=jnp.bfloat16):
    loudness = level_of(rng, shape, pieces, -0.22, 0.18) if pieces else 1.0
    drawn = jax.random.normal(rng, shape, jnp.float32) * width * loudness
    return jnp.minimum(jnp.maximum(drawn, -limit), limit).astype(kind)


def setup_inputs(seed: int = 0) -> dict:
    arg_keys = jax.random.split(jax.random.key(seed), 9)
    state = scatter_about(arg_keys[0], (2, MEMBERS, EMITTERS), 0.5, 3.0, ((2, 256),), jnp.float32)
    prev_slope = scatter_about(arg_keys[1], (2, MEMBERS, EMITTERS), 0.6, 4.0, ((2, 256),), jnp.float32)
    positions = jnp.clip(jax.random.uniform(arg_keys[2], (2, EMITTERS), jnp.float32, -1.0, 1.0) * level_of(arg_keys[2], (2, EMITTERS), ((1, 256),), -0.4, 0.0), -1.0, 1.0)
    pump = jnp.clip(-0.5 + 2.0 * jax.random.uniform(arg_keys[3], (EMITTERS,), jnp.float32) ** level_of(arg_keys[3], (EMITTERS,), ((0, 256),), -0.2, 0.2), -0.5, 1.5)
    detuning = scatter_about(arg_keys[4], (EMITTERS,), 1.0, 4.0, ((0, 256),), jnp.float32)
    kappa = jnp.clip(jnp.exp(math.log(1.0) - 1.609438 * jax.random.uniform(arg_keys[5], (NEIGH, EMITTERS), jnp.float32) ** level_of(arg_keys[5], (NEIGH, EMITTERS), ((1, 256),), -0.2, 0.2)), 0.2, 1.0)
    neighbours = with_ends(jax.random.randint(arg_keys[6], (NEIGH, EMITTERS), 0, ROWS + 2 * HALO), jax.random.fold_in(arg_keys[6], 1), 0, (ROWS + 2 * HALO) - 1).astype(jnp.int32)
    send_list = with_ends(jax.random.randint(arg_keys[7], (2, HALO * DEVICES), 0, ROWS), jax.random.fold_in(arg_keys[7], 1), 0, ROWS - 1).astype(jnp.int32)
    return dict(state=state, prev_slope=prev_slope, positions=positions, pump=pump, detuning=detuning, kappa=kappa, neighbours=neighbours, send_list=send_list)


section_weight = 0.25
phase_rate = 60.0
alpha_factor = 2.0

def kernel_table(source_place, target_place, scaled):
    horizontal = target_place[0][None, :] - source_place[0][:, None]
    vertical = target_place[1][None, :] - source_place[1][:, None]
    phase = phase_rate * (horizontal * horizontal + vertical * vertical)
    cosine = (scaled * jnp.cos(phase)).astype(jnp.bfloat16)
    sine_part = (scaled * jnp.sin(phase)).astype(jnp.bfloat16)
    return jnp.concatenate([cosine, sine_part], axis=1)

def block_columns(total, fields, source_place, target_place, scaled):
    members = fields.shape[1]
    targets = target_place.shape[1]
    kernel = kernel_table(source_place, target_place, scaled)
    flat = fields.reshape(2 * members, fields.shape[2])
    product = jnp.dot(flat, kernel, preferred_element_type=jnp.float32)
    real_part = product[:members, :targets] - product[members:, targets:]
    imag_part = product[:members, targets:] + product[members:, :targets]
    return total + jnp.stack([real_part, imag_part])

def reference(state, prev_slope, positions, pump, detuning, kappa, neighbours, send_list):
    section_field = state + section_weight * prev_slope
    section_half = section_field.astype(jnp.bfloat16)
    scaled = 1.0 / math.sqrt(EMITTERS)

    def one_block(block_index, total):
        fields = lax.dynamic_slice_in_dim(section_half, block_index * ROWS, ROWS, 2)
        source_place = lax.dynamic_slice_in_dim(positions, block_index * ROWS, ROWS, 1)
        return block_columns(total, fields, source_place, positions, scaled)
    empty = jnp.zeros((2, MEMBERS, EMITTERS), jnp.float32)
    fresnel = lax.fori_loop(0, DEVICES, one_block, empty)
    blocked = section_field.reshape(2, MEMBERS, DEVICES, ROWS)
    lists = send_list.reshape(2, DEVICES, HALO)
    next_index = jnp.broadcast_to(lists[0][None, None], (2, MEMBERS, DEVICES, HALO))
    prev_index = jnp.broadcast_to(lists[1][None, None], (2, MEMBERS, DEVICES, HALO))
    to_next = jnp.take_along_axis(blocked, next_index, axis=3)
    to_prev = jnp.take_along_axis(blocked, prev_index, axis=3)
    zero_block = jnp.zeros((2, MEMBERS, 1, HALO), jnp.float32)
    from_prev = jnp.concatenate([zero_block, to_next[:, :, :-1]], axis=2)
    from_next = jnp.concatenate([to_prev[:, :, 1:], zero_block], axis=2)
    whole_buffer = jnp.concatenate([blocked, from_prev, from_next], axis=3)
    neighbour_blocks = neighbours.reshape(NEIGH, DEVICES, ROWS)
    coupled = jnp.zeros((2, MEMBERS, EMITTERS), jnp.float32)
    for neighbour_slot in range(NEIGH):
        index_full = jnp.broadcast_to(neighbour_blocks[neighbour_slot][None, None], (2, MEMBERS, DEVICES, ROWS))
        picked = jnp.take_along_axis(whole_buffer, index_full, axis=3).reshape(2, MEMBERS, EMITTERS)
        coupled = coupled + kappa[neighbour_slot] * picked
    real_field = section_field[0]
    imag_field = section_field[1]
    modulus = real_field * real_field + imag_field * imag_field
    linear_real = pump - modulus
    linear_imag = detuning - alpha_factor * modulus
    local_real = linear_real * real_field - linear_imag * imag_field
    local_imag = linear_real * imag_field + linear_imag * real_field
    slope_real = local_real + fresnel[0] - coupled[1]
    slope_imag = local_imag + fresnel[1] + coupled[0]
    return jnp.stack([slope_real, slope_imag])
```

```python
import math

import jax
import jax.numpy as jnp
from jax import lax
from jax.experimental import pallas as pl
from jax.experimental.pallas import tpu as pltpu
from jax.sharding import PartitionSpec as P

section_weight = 0.25
phase_rate = 60.0
alpha_factor = 2.0

MESH = pl.DeviceIdType.MESH
ROOT_HALF = 2.0**-0.5
MAGIC = 12582912.0
SINE = tuple(2.0**0.25 * c for c in (3.14158202, -5.1671428, 2.54189902, -0.55463618))


def place():
    band, member = lax.axis_index("blk"), lax.axis_index("grp")
    return band // 2, (member // 2) % 2 * 2 + band % 2, member // 4, member % 2


def device(z, y, x, core):
    return (z * 2 + y % 2, x * 4 + y // 2 * 2 + core)


def column_peer(k):
    z, y, x, core = place()
    return device((z + k // 2) % 8, y, x, (core + k) % 2)


def plane_peer(k, sign=1):
    z, y, x, core = place()
    return device(z, (y + sign * (k % 4)) % 4, (x + sign * (k // 4)) % 4, core)


def listed_peer(step):
    index = (lax.axis_index("blk") * 16 + lax.axis_index("grp") + step) % 256
    return (index // 16, index % 16)


def wave(turns):
    f = turns - jnp.round(turns)
    z = f * f
    p = SINE[3] * z + SINE[2]
    p = p * z + SINE[1]
    p = p * z + SINE[0]
    u = f * p
    w = u * u
    a = 2.0 * ROOT_HALF - w
    return ROOT_HALF - w, (u * a) * lax.rsqrt(a)


def exact_dot(a, b):
    return jnp.dot(a, b, precision=lax.Precision.HIGHEST, preferred_element_type=jnp.float32)


def kernel(
    state, prev_slope, positions, pump, detuning, kappa, neighbours, send_list, out,
    fields, source_at, target_at, table, partial, arrived, own_sum, listed, halo,
    f_send, f_recv, s_send, s_recv, t_send, t_recv, p_send, p_recv, h_send, h_recv,
):
    n = 128
    barrier = pltpu.get_barrier_semaphore()
    for k in range(1, 16):
        pl.semaphore_signal(barrier, inc=1, device_id=column_peer(k), device_id_type=MESH)
        pl.semaphore_signal(barrier, inc=1, device_id=plane_peer(k), device_id_type=MESH)
    for step in (1, 255):
        pl.semaphore_signal(barrier, inc=1, device_id=listed_peer(step), device_id_type=MESH)

    field = [state[i] + section_weight * prev_slope[i] for i in range(2)]
    field_t = jnp.concatenate([field[0].T, field[1].T], axis=1)
    fields[pl.ds(0, n), :] = field_t.astype(jnp.bfloat16)
    scaled = positions[...] * math.sqrt(phase_rate / (2.0 * math.pi))
    source_at[0] = scaled
    target_at[0] = scaled
    lists = jnp.concatenate([send_list[0:1, :], send_list[1:2, :]], axis=1)
    rows = lax.broadcasted_iota(jnp.int32, (n, n), 0)
    chosen = jnp.where(rows == lists, 1.0, 0.0)
    listed[...] = exact_dot(chosen.T, field_t)

    pl.semaphore_wait(barrier, 32)

    pending = []

    def send(src, dst, send_sem, recv_sem, peer):
        copy = pltpu.make_async_remote_copy(
            src_ref=src, dst_ref=dst, send_sem=send_sem, recv_sem=recv_sem, device_id=peer, device_id_type=MESH
        )
        copy.start()
        pending.append(copy)
        return copy

    def block(k):
        return fields.at[pl.ds(k * n, n)]

    s_copies, t_copies = {}, {}
    for k in range(1, 16):
        s_copies[k] = send(source_at.at[0], source_at.at[k], s_send.at[k], s_recv.at[k], column_peer(k))
        t_copies[k] = send(target_at.at[0], target_at.at[k], t_send.at[k], t_recv.at[k], plane_peer(k, -1))
    f_copies = {1: send(block(0), block(1), f_send.at[1], f_recv.at[1], column_peer(1))}
    for step in (1, 7, 2, 6, 3, 5, 4):
        k = 2 * step
        f_copies[k] = send(block(0), block(k), f_send.at[k], f_recv.at[k], column_peer(k))
    h_copies = [
        send(listed.at[pl.ds(i * 64, 64)], halo.at[pl.ds(i * 64, 64)], h_send.at[i], h_recv.at[i], listed_peer(step))
        for i, step in enumerate((1, 255))
    ]

    for k in range(1, 16):
        s_copies[k].wait_recv()
        t_copies[k].wait_recv()

    def tabulate(i, _):
        t, s = i // 4, i % 4 * 4
        tx = jnp.broadcast_to(target_at[t, 0:1, :], (n, n)).T
        ty = jnp.broadcast_to(target_at[t, 1:2, :], (n, n)).T
        for j in range(4):
            dx = tx - source_at[s + j, 0:1, :]
            dy = ty - source_at[s + j, 1:2, :]
            cosine, sine = wave(dx * dx + dy * dy)
            at = pl.multiple_of((s + j) * n, n)
            table[t, :, pl.ds(at, n)] = cosine.astype(jnp.bfloat16)
            table[t, :, pl.ds(16 * n + at, n)] = sine.astype(jnp.bfloat16)
        return 0

    lax.fori_loop(0, 64, tabulate, 0)

    for step in (1, 7, 2, 6, 3, 5, 4):
        k = 2 * step
        f_copies[k].wait_recv()
        f_copies[k + 1] = send(block(k), block(k + 1), f_send.at[k + 1], f_recv.at[k + 1], column_peer(1))
    for step in range(8):
        f_copies[2 * step + 1].wait_recv()

    def turned(k, _):
        here = fields[pl.ds(pl.multiple_of(k * n, n), n), :]
        fields[pl.ds(pl.multiple_of((k + 16) * n, n), n), :] = jnp.concatenate([-here[:, n:], here[:, :n]], axis=1)
        return 0

    lax.fori_loop(0, 16, turned, 0)

    def total(t):
        return jnp.dot(table[t], fields[...], preferred_element_type=jnp.float32)

    r_copies = []
    for t in range(1, 16):
        partial[t] = total(t).astype(jnp.bfloat16)
        r_copies.append(send(partial.at[t], arrived.at[t], p_send.at[t], p_recv.at[t], plane_peer(t)))
    own_sum[...] = total(0)

    for copy in h_copies:
        copy.wait_recv()
    index = lax.axis_index("blk") * 16 + lax.axis_index("grp")
    places = lax.broadcasted_iota(jnp.int32, (2 * n, n), 0)
    mixing = jnp.zeros((2 * n, n), jnp.float32)
    for slot in range(6):
        mixing += jnp.where(places == neighbours[slot : slot + 1, :], kappa[slot : slot + 1, :], 0.0)
    first = jnp.where(index == 0, 0.0, 1.0)
    last = jnp.where(index == 255, 0.0, 1.0)
    mixing_halo = mixing[n:] * jnp.where(rows < 64, first, last)
    halo_t = halo[...]
    for i in range(2):
        coupled = exact_dot(field[i], mixing[:n]) + exact_dot(halo_t[:, i * n : (i + 1) * n].T, mixing_halo)
        out[1 - i] = coupled if i == 0 else -coupled
    modulus = field[0] * field[0] + field[1] * field[1]
    linear_real = pump[...] - modulus
    linear_imag = detuning[...] - alpha_factor * modulus
    out[0] += linear_real * field[0] - linear_imag * field[1]
    out[1] += linear_real * field[1] + linear_imag * field[0]

    for copy in r_copies:
        copy.wait_recv()
    fresnel = own_sum[...]
    for t in range(1, 16):
        fresnel += arrived[t].astype(jnp.float32)
    fresnel = fresnel * 2.0**-7
    for i in range(2):
        out[i] += fresnel[:, i * n : (i + 1) * n].T
    for copy in pending:
        copy.wait_send()


def local(state, prev_slope, positions, pump, detuning, kappa, neighbours, send_list):
    dma = pltpu.SemaphoreType.DMA
    return pl.pallas_call(
        kernel,
        out_shape=jax.ShapeDtypeStruct(state.shape, jnp.float32),
        in_specs=[pl.BlockSpec(memory_space=pltpu.VMEM)] * 8,
        out_specs=pl.BlockSpec(memory_space=pltpu.VMEM),
        scratch_shapes=[
            pltpu.VMEM((4096, 256), jnp.bfloat16),
            pltpu.VMEM((16, 2, 128), jnp.float32),
            pltpu.VMEM((16, 2, 128), jnp.float32),
            pltpu.VMEM((16, 128, 4096), jnp.bfloat16),
            pltpu.VMEM((16, 128, 256), jnp.bfloat16),
            pltpu.VMEM((16, 128, 256), jnp.bfloat16),
            pltpu.VMEM((128, 256), jnp.float32),
            pltpu.VMEM((128, 256), jnp.float32),
            pltpu.VMEM((128, 256), jnp.float32),
        ]
        + [dma((16,))] * 8
        + [dma((2,))] * 2,
        compiler_params=pltpu.CompilerParams(
            collective_id=0, has_side_effects=True, vmem_limit_bytes=48 * 2**20
        ),
    )(state, prev_slope, positions, pump.reshape(1, -1), detuning.reshape(1, -1), kappa, neighbours, send_list)


def solution(mesh):
    last, flat = P(None, ("blk", "grp")), P(("blk", "grp"))
    whole = P(None, None, ("blk", "grp"))
    return jax.shard_map(
        local,
        mesh=mesh,
        in_specs=(whole, whole, last, flat, flat, last, last, last),
        out_specs=whole,
        check_vma=False,
    )
```
